32 devices in a mesh: parts: 2 (over x), node: 2 (over core), lane: 8 (over z, y).
Axes of the slice: x: 2, y: 2, z: 4, core: 2. Of those that a mesh axis runs over, the one named last changes fastest.
Arguments:
- quant_rows: bfloat16 [1024, 7168], P(('parts', 'node', 'lane')), parts along dimension 0, may hold values from -6 to 6
- block_scales: bfloat16 [1024, 56], P(('parts', 'node', 'lane')), parts along dimension 0, may hold values from 0.5 to 2
- expert_ids: int32 [1024, 4], P(('parts', 'node', 'lane')), parts along dimension 0, may hold values from 0 to 7, all different within a row; in each aligned block of 32 rows (0 to 31, 32 to 63, ...) at most 24 rows name the same one
- route_gates: bfloat16 [1024, 4], P(('parts', 'node', 'lane')), parts along dimension 0, may hold values from 0.19921875 to 1
- gate_proj: bfloat16 [16, 7168, 1024], P(('node', 'lane')), may hold values from -0.0625 to 0.0625
- up_proj: bfloat16 [16, 7168, 1024], P(('node', 'lane')), may hold values from -0.0625 to 0.0625
- down_proj: bfloat16 [16, 1024, 7168], P(('node', 'lane')), may hold values from -0.125 to 0.125
Outputs:
- moe_output: bfloat16 [1024, 7168], P(('parts', 'node', 'lane')), parts along dimension 0
The draws below stay inside these ranges and needn't reach their ends.
There are 2 independent parts, one for each index of `parts`. The reference program is written for one: setup_inputs(seed, part) draws one part's arguments, and reference() takes and returns one part's arrays. A program takes and returns all parts, laid end to end along the dimension named above; an argument that names none is the same for every part. Nothing has to cross between parts.
Inputs may be any that keep to these rules, and one draw needn't show every extreme that they name: `expert_ids`: each row names 4 different experts. Among the 32 rows of one device no expert is named by more than 24 rows, and in every draw some device has an expert named by exactly 24 of its rows.
All inputs are finite; a program needn't handle non-finite values.
Results may differ from the reference program's by a relative error of at most 0.012.
Values may be sent and summed in bfloat16 or wider, within the bound.
A program may use at most 192 MiB of HBM per device.

```python
import math
import jax
import jax.numpy as jnp
import numpy as np
from jax import lax

D = 7168
FF = 2048
BLOCK = 128
TOPK = 4
EXP_GRP = 4
ROWS = 32
CAP = 24
SPAN = 2
H_DEV = 1024
EXPERTS = 8
TOKENS = 512
SCALE_BLOCKS = 56
N_LANE = 8


def shard_levels(own_key, dims, cuts, low, top_value):
    level, own = 1.0, jax.random.fold_in(own_key, 6)
    for axis_at, blocks in cuts:
        draws = jnp.exp(jax.random.uniform(jax.random.fold_in(own, axis_at), (blocks,), jnp.float32, low / len(cuts), top_value / len(cuts)))
        level = level * jnp.repeat(draws, dims[axis_at] // blocks).reshape([-1 if axis == axis_at else 1 for axis in range(len(dims))])
    return level


def shared_out(own_key, own, number, rows, amount, top, reach, lean):
    order = jax.random.permutation(own_key, amount)
    packed, ordinary = load_shares(amount, rows * top, reach, lean, True), load_shares(amount, rows * top, reach, lean, False)
    places = jnp.arange(amount)

    def named(lengths, turn):
        used = int((lengths > 0).sum())
        fixed = max(1, used // 4)
        moved = fixed + (places - fixed + turn * (used - fixed)) % max(1, amount - fixed)
        return jnp.zeros((amount,), jnp.int32).at[order[jnp.where(places < fixed, places, moved)]].set(jnp.asarray(lengths, jnp.int32))

    lengths = jnp.where(number % 4 == 0, named(packed, number // 4), named(ordinary, number - number // 4 - 1))
    mixed = jax.random.permutation(jax.random.fold_in(own, 3), amount)
    source_of, receiver = mixed[0:amount // 2 * 2:2], mixed[1:amount // 2 * 2:2]
    margin = jnp.minimum(lengths[source_of] - 1, reach - lengths[receiver]) // 2
    margin = jnp.where((source_of == order[0]) | (receiver == order[0]) | (lengths[receiver] == 0), 0, jnp.maximum(margin, 0))
    moved = jax.random.randint(jax.random.fold_in(own, 4), (amount // 2,), 0, 1 << 20) % (margin + 1)
    lengths = lengths.at[source_of].add(-moved).at[receiver].add(moved)
    members = jnp.searchsorted(jnp.cumsum(lengths), jnp.arange(rows * top), side="right").astype(jnp.int32)
    listing = members.reshape(top, rows).T
    listing = listing[jax.random.permutation(jax.random.fold_in(own, 1), rows)]
    turn = jax.random.randint(jax.random.fold_in(own, 2), (rows, 1), 0, top)
    return jnp.take_along_axis(listing, (jnp.arange(top)[None, :] + turn) % top, axis=1)


def load_shares(amount, total, bound, lean, full):
    portions = [(1 << 20) // math.isqrt(rank ** lean) + 1 for rank in range(1, amount + 1)]
    largest = bound if full else min(bound, max(-(-total // amount), total * portions[0] // sum(portions)))
    least = 1 if total - largest >= amount - 1 else 0
    given, surplus = [largest] + [least] * (amount - 1), total - largest - least * (amount - 1)
    while surplus > 0:
        free = [i for i in range(1, amount) if given[i] < largest] or [i for i in range(1, amount) if given[i] < bound]
        whole, remaining = sum([portions[i] for i in free]), surplus
        for i in free:
            more = min(bound - given[i], max(1, remaining * portions[i] // whole), surplus)
            given[i] = given[i] + more
            surplus = surplus - more
    return np.array(given)


def scatter_about(key, dims, width, bound, split=(), held_as=jnp.bfloat16):
    entries = width * jax.random.normal(key, dims, jnp.float32)
    if split:
        entries = entries * shard_levels(key, dims, split, -0.22, 0.18)
    return jnp.clip(entries, -bound, bound).astype(held_as)


def setup_inputs(seed: int = 0, part: int = 0) -> dict:
    splits = jax.random.split(jax.random.key(seed), 8)
    part_splits = jax.random.split(jax.random.fold_in(splits[7], part), 8)
    quant_rows = scatter_about(part_splits[0], (TOKENS, D), 1.0, 6.0, ((0, 16),))
    block_scales = jnp.clip(jnp.exp(math.log(2.0) - 1.3862944 * jax.random.uniform(part_splits[1], (TOKENS, SCALE_BLOCKS), jnp.float32) ** shard_levels(part_splits[1], (TOKENS, SCALE_BLOCKS), ((0, 16),), -0.2, 0.2)), 0.5, 2.0).astype(jnp.bfloat16)
    expert_ids_keys = jax.random.split(jax.random.fold_in(part_splits[2], 1), TOKENS // ROWS)
    expert_ids_turns = jax.random.permutation(jax.random.fold_in(part_splits[2], 3), TOKENS // ROWS)
    expert_ids = jax.vmap(lambda own, number: shared_out(jax.random.fold_in(part_splits[2], 2), own, number, ROWS, EXPERTS, TOPK, CAP, 2))(expert_ids_keys, expert_ids_turns).reshape((TOKENS, TOPK))
    route_gates = jnp.clip(0.19921875 + 0.80078125 * jax.random.uniform(part_splits[3], (TOKENS, TOPK), jnp.float32) ** shard_levels(part_splits[3], (TOKENS, TOPK), ((0, 16),), -0.2, 0.2), 0.19921875, 1.0).astype(jnp.bfloat16)
    gate_proj = scatter_about(splits[4], (EXPERTS * SPAN, D, H_DEV), D ** -0.5, 0.0625, ((0, 16),))
    up_proj = scatter_about(splits[5], (EXPERTS * SPAN, D, H_DEV), D ** -0.5, 0.0625, ((0, 16),))
    down_proj = scatter_about(splits[6], (EXPERTS * SPAN, H_DEV, D), FF ** -0.5, 0.125, ((0, 16),))
    return {"quant_rows": quant_rows, "block_scales": block_scales, "expert_ids": expert_ids, "route_gates": route_gates, "gate_proj": gate_proj, "up_proj": up_proj, "down_proj": down_proj}


def reference(quant_rows, block_scales, expert_ids, route_gates, gate_proj, up_proj, down_proj):
    span_count = N_LANE // EXP_GRP
    block_total = D // BLOCK
    scaled = quant_rows.astype(jnp.float32).reshape(TOKENS, block_total, BLOCK) * block_scales.astype(jnp.float32)[:, :, None]
    inputs = scaled.reshape(TOKENS, D).astype(jnp.bfloat16)
    labels = jnp.arange(EXPERTS, dtype=jnp.int32)
    weights = jnp.sum(jnp.where(expert_ids[:, :, None] == labels[None, None, :], route_gates.astype(jnp.float32)[:, :, None], jnp.float32(0.0)), axis=1)

    def add_slice(running, slice_index):
        expert = slice_index // span_count
        gate_out = jnp.dot(inputs, gate_proj[slice_index], preferred_element_type=jnp.float32)
        up_out = jnp.dot(inputs, up_proj[slice_index], preferred_element_type=jnp.float32)
        hidden = (jax.nn.silu(gate_out) * up_out).astype(jnp.bfloat16)
        projected = jnp.dot(hidden, down_proj[slice_index], preferred_element_type=jnp.float32)
        column = lax.dynamic_index_in_dim(weights, expert, 1, keepdims=False)
        slice_term = (column[:, None] * projected).astype(jnp.bfloat16)
        slice_term = lax.optimization_barrier(slice_term)
        return running + slice_term.astype(jnp.float32), None

    running, _ = lax.scan(add_slice, jnp.zeros((TOKENS, D), jnp.float32), jnp.arange(EXPERTS * span_count, dtype=jnp.int32))
    return running.astype(jnp.bfloat16)
```

```python
import functools

import jax
import jax.numpy as jnp
from jax import lax
from jax.experimental import pallas as pl
from jax.experimental.pallas import tpu as pltpu
from jax.sharding import PartitionSpec as P

EXP_GRP = 4
Y = 2
CORES = 2
LANES = 128
TILE = 256
MESH = pl.DeviceIdType.MESH
F32 = jnp.float32
BF16 = jnp.bfloat16


def flip(value, bit):
    return value + bit - 2 * bit * ((value // bit) % 2)


def flip_all(value, mask):
    bit = 1
    while bit <= mask:
        if mask & bit:
            value = flip(value, bit)
        bit *= 2
    return value


def kernel(
    planes, pieces, span_count,
    quant_ref, scale_ref, ids_ref, gates_ref, gate_hbm, up_hbm, down_hbm,
    out_ref,
    gate_w, up_w, down_w, rows_buf, hidden, from_core, from_y, from_z,
    gate_sem, up_sem, down_sem,
    gz_send, gz_recv, gy_send, gy_recv, gc_send, gc_recv,
    rc_send, rc_recv, ry_send, ry_recv, rz_send, rz_recv,
):
    own, width = quant_ref.shape
    units = gate_w.shape[1]
    tiles = units // TILE
    group = CORES * Y * own
    part = width // pieces
    node, lane = lax.axis_index("node"), lax.axis_index("lane")
    z, y = lane // Y, lane % Y
    expert = node * EXP_GRP + lane // span_count

    def lane_z(mask):
        return {"lane": flip_all(z, mask) * Y + y}

    lane_y = {"lane": z * Y + (1 - y)}
    other_core = {"node": 1 - node}

    def weight_copies(j):
        cols = pl.ds(j * TILE, TILE)
        return (
            pltpu.make_async_copy(gate_hbm.at[0, :, cols], gate_w.at[:, cols], gate_sem.at[j]),
            pltpu.make_async_copy(up_hbm.at[0, :, cols], up_w.at[:, cols], up_sem.at[j]),
        )

    def down_copy(j):
        cols = pl.ds(j * part, part)
        return pltpu.make_async_copy(down_hbm.at[0, :, cols], down_w.at[:, cols], down_sem.at[j])

    for j in range(tiles):
        for copy in weight_copies(j):
            copy.start()
    for j in range(pieces):
        down_copy(j).start()

    barrier = pltpu.get_barrier_semaphore()
    for mask in range(1, planes):
        pl.semaphore_signal(barrier, inc=1, device_id=lane_z(mask), device_id_type=MESH)
    pl.semaphore_signal(barrier, inc=1, device_id=lane_y, device_id_type=MESH)
    pl.semaphore_signal(barrier, inc=1, device_id=other_core, device_id_type=MESH)

    labels = lax.broadcasted_iota(jnp.int32, (own, LANES), 1)
    route = jnp.zeros((own, LANES), F32)
    for k in range(ids_ref.shape[1]):
        route += jnp.where(
            ids_ref[:, k:k + 1] == labels, gates_ref[:, k:k + 1].astype(F32), 0.0
        )
    rows_buf[0:own, width:width + LANES] = route.astype(BF16)
    block = width // scale_ref.shape[1]
    for j in range(scale_ref.shape[1]):
        cols = slice(j * block, (j + 1) * block)
        rows_buf[0:own, cols] = (
            quant_ref[:, cols].astype(F32) * scale_ref[:, j:j + 1].astype(F32)
        ).astype(BF16)

    pl.semaphore_wait(barrier, planes - 1 + 2)

    def slot(g, c, v):
        return pl.ds(g * group + (c * Y + v) * own, own)

    def gz(g):
        bit = g & -g
        return pltpu.make_async_remote_copy(
            src_ref=rows_buf.at[slot(g ^ bit, 0, 0)], dst_ref=rows_buf.at[slot(g, 0, 0)],
            send_sem=gz_send.at[g], recv_sem=gz_recv.at[g],
            device_id=lane_z(bit), device_id_type=MESH)

    def gy(g):
        return pltpu.make_async_remote_copy(
            src_ref=rows_buf.at[slot(g, 0, 0)], dst_ref=rows_buf.at[slot(g, 0, 1)],
            send_sem=gy_send.at[g], recv_sem=gy_recv.at[g],
            device_id=lane_y, device_id_type=MESH)

    def gc(g, v):
        return pltpu.make_async_remote_copy(
            src_ref=rows_buf.at[slot(g, 0, v)], dst_ref=rows_buf.at[slot(g, 1, v)],
            send_sem=gc_send.at[g * Y + v], recv_sem=gc_recv.at[g * Y + v],
            device_id=other_core, device_id_type=MESH)

    def children(g):
        low = g & -g if g else planes
        bit, found = 1, []
        while bit < low and g + bit < planes:
            found.append(g + bit)
            bit *= 2
        return found

    def spread(g):
        if g:
            gz(g).wait_recv()
        for child in children(g):
            gz(child).start()
        gy(g).start()
        gc(g, 0).start()

    def pass_on(g):
        gy(g).wait_recv()
        gc(g, 1).start()

    def sends_done(g):
        for child in children(g):
            gz(child).wait_send()
        gy(g).wait_send()
        for v in range(Y):
            gc(g, v).wait_send()

    def cols_of(p):
        return pl.ds(p * part, part)

    def rc(g, p):
        return pltpu.make_async_remote_copy(
            src_ref=rows_buf.at[pl.ds(g * group + Y * own, Y * own), cols_of(p)],
            dst_ref=from_core.at[pl.ds(g * Y * own, Y * own), cols_of(p)],
            send_sem=rc_send.at[g * pieces + p], recv_sem=rc_recv.at[g * pieces + p],
            device_id=other_core, device_id_type=MESH)

    def ry(g, p):
        return pltpu.make_async_remote_copy(
            src_ref=rows_buf.at[slot(g, 0, 1), cols_of(p)],
            dst_ref=from_y.at[pl.ds(g * own, own), cols_of(p)],
            send_sem=ry_send.at[g * pieces + p], recv_sem=ry_recv.at[g * pieces + p],
            device_id=lane_y, device_id_type=MESH)

    def rz(g, p):
        return pltpu.make_async_remote_copy(
            src_ref=rows_buf.at[slot(g, 0, 0), cols_of(p)],
            dst_ref=from_z.at[pl.ds((g - 1) * own, own), cols_of(p)],
            send_sem=rz_send.at[(g - 1) * pieces + p], recv_sem=rz_recv.at[(g - 1) * pieces + p],
            device_id=lane_z(g), device_id_type=MESH)

    def add(rows, more, more_rows, p):
        @pl.loop(0, part // TILE)
        def _(i):
            cols = pl.ds(pl.multiple_of(p * part + i * TILE, TILE), TILE)
            rows_buf[rows, cols] = (
                rows_buf[rows, cols].astype(F32) + more[more_rows, cols].astype(F32)
            ).astype(BF16)

    def core_sum(g, p):
        rc(g, p).wait_recv()
        add(slot(g, 0, 1), from_core, pl.ds((g * Y + 1) * own, own), p)
        ry(g, p).start()
        add(slot(g, 0, 0), from_core, pl.ds(g * Y * own, own), p)

    def y_sum(g, p):
        ry(g, p).wait_recv()
        add(slot(g, 0, 0), from_y, pl.ds(g * own, own), p)
        if g:
            rz(g, p).start()

    def gate_up(g):
        for v in range(Y):
            gc(g, v).wait_recv()
        rows = pl.ds(g * group, group)
        if g == 0:
            for j in range(tiles):
                for copy in weight_copies(j):
                    copy.wait()

        @pl.loop(0, tiles)
        def _(j):
            cols = pl.ds(pl.multiple_of(j * TILE, TILE), TILE)
            x = rows_buf[rows, 0:width]
            gate = jnp.dot(x, gate_w[:, cols], preferred_element_type=F32)
            up = jnp.dot(x, up_w[:, cols], preferred_element_type=F32)
            hidden[:, cols] = (gate / (1.0 + jnp.exp(-gate)) * up).astype(BF16)

    def project(g):
        sends_done(g)
        rows = pl.ds(g * group, group)
        route_all = rows_buf[rows, width:width + LANES].astype(F32)
        spots = lax.broadcasted_iota(jnp.int32, (group, LANES), 1)
        column = jnp.sum(jnp.where(spots == expert, route_all, 0.0), axis=1, keepdims=True)
        for p in range(pieces):
            if g == 0:
                down_copy(p).wait()

            @pl.loop(0, part // TILE)
            def _(i):
                cols = pl.ds(pl.multiple_of(p * part + i * TILE, TILE), TILE)
                term = jnp.dot(hidden[...], down_w[:, cols], preferred_element_type=F32)
                rows_buf[rows, cols] = (column * term).astype(BF16)

            rc(g, p).start()

    spread(0)
    for g in range(1, min(planes, 3)):
        spread(g)
    pass_on(0)
    for g in range(planes):
        gate_up(g)
        if g + 1 < planes:
            pass_on(g + 1)
        if 2 < g + 3 < planes:
            spread(g + 3)
        if g >= 1:
            for p in range(pieces):
                core_sum(g - 1, p)
        project(g)
        if g >= 1:
            for p in range(pieces):
                y_sum(g - 1, p)
    last = planes - 1
    for p in range(pieces):
        core_sum(last, p)
    for p in range(pieces):
        y_sum(last, p)
    for p in range(pieces):
        for g in range(1, planes):
            rz(g, p).wait_recv()

        @pl.loop(0, part // TILE)
        def _(i):
            cols = pl.ds(pl.multiple_of(p * part + i * TILE, TILE), TILE)
            total = rows_buf[0:own, cols].astype(F32)
            for g in range(1, planes):
                total += from_z[(g - 1) * own:g * own, cols].astype(F32)
            out_ref[:, cols] = total.astype(BF16)

    for g in range(planes):
        for p in range(pieces):
            rc(g, p).wait_send()
            ry(g, p).wait_send()
            if g:
                rz(g, p).wait_send()


def local(quant_rows, block_scales, expert_ids, route_gates, gate_proj, up_proj, down_proj):
    lane_total = lax.axis_size("lane")
    planes = lane_total // Y
    span_count = lane_total // EXP_GRP
    own, width = quant_rows.shape
    units = gate_proj.shape[2]
    pieces = 4
    rows = planes * Y * CORES * own
    dma = pltpu.SemaphoreType.DMA
    vmem = pl.BlockSpec(memory_space=pltpu.VMEM)
    hbm = pl.BlockSpec(memory_space=pl.ANY)
    return pl.pallas_call(
        functools.partial(kernel, planes, pieces, span_count),
        out_shape=jax.ShapeDtypeStruct((own, width), BF16),
        in_specs=[vmem] * 4 + [hbm] * 3,
        out_specs=vmem,
        scratch_shapes=[
            pltpu.VMEM((width, units), BF16),
            pltpu.VMEM((width, units), BF16),
            pltpu.VMEM((units, width), BF16),
            pltpu.VMEM((rows, width + LANES), BF16),
            pltpu.VMEM((Y * CORES * own, units), BF16),
            pltpu.VMEM((planes * Y * own, width), BF16),
            pltpu.VMEM((planes * own, width), BF16),
            pltpu.VMEM(((planes - 1) * own, width), BF16),
            dma((units // TILE,)), dma((units // TILE,)), dma((pieces,)),
            dma((planes,)), dma((planes,)),
            dma((planes,)), dma((planes,)),
            dma((planes * Y,)), dma((planes * Y,)),
            dma((planes * pieces,)), dma((planes * pieces,)),
            dma((planes * pieces,)), dma((planes * pieces,)),
            dma((planes * pieces,)), dma((planes * pieces,)),
        ],
        compiler_params=pltpu.CompilerParams(
            collective_id=0, has_side_effects=True, vmem_limit_bytes=62 << 20
        ),
    )(quant_rows, block_scales, expert_ids, route_gates, gate_proj, up_proj, down_proj)


def solution(mesh):
    rows = P(("parts", "node", "lane"), None)
    weights = P(("node", "lane"), None, None)
    return jax.shard_map(
        local,
        mesh=mesh,
        in_specs=(rows,) * 4 + (weights,) * 3,
        out_specs=rows,
        check_vma=False,
    )
```

```python
import functools

import jax
import jax.numpy as jnp
from jax import lax
from jax.experimental import pallas as pl
from jax.experimental.pallas import tpu as pltpu
from jax.sharding import PartitionSpec as P

EXP_GRP = 4
Y = 2
CORES = 2
LANES = 128
TILE = 256
MESH = pl.DeviceIdType.MESH
F32 = jnp.float32
BF16 = jnp.bfloat16


def flip(value, bit):
    return value + bit - 2 * bit * ((value // bit) % 2)


def flip_all(value, mask):
    bit = 1
    while bit <= mask:
        if mask & bit:
            value = flip(value, bit)
        bit *= 2
    return value


def kernel(
    planes, pieces, span_count,
    quant_ref, scale_ref, ids_ref, gates_ref, gate_hbm, up_hbm, down_hbm,
    out_ref,
    gate_w, up_w, down_w, rows_buf, hidden, from_core, from_y, from_z,
    gate_sem, up_sem, down_sem,
    gz_send, gz_recv, gy_send, gy_recv, gc_send, gc_recv,
    rc_send, rc_recv, ry_send, ry_recv, rz_send, rz_recv,
):
    own, width = quant_ref.shape
    units = gate_w.shape[1]
    tiles = units // TILE
    group = CORES * Y * own
    part = width // pieces
    node, lane = lax.axis_index("node"), lax.axis_index("lane")
    z, y = lane // Y, lane % Y
    expert = node * EXP_GRP + lane // span_count

    def lane_z(mask):
        return {"lane": flip_all(z, mask) * Y + y}

    lane_y = {"lane": z * Y + (1 - y)}
    other_core = {"node": 1 - node}

    def weight_copies(j):
        cols = pl.ds(j * TILE, TILE)
        return (
            pltpu.make_async_copy(gate_hbm.at[0, :, cols], gate_w.at[:, cols], gate_sem.at[j]),
            pltpu.make_async_copy(up_hbm.at[0, :, cols], up_w.at[:, cols], up_sem.at[j]),
        )

    def down_copy(j):
        cols = pl.ds(j * part, part)
        return pltpu.make_async_copy(down_hbm.at[0, :, cols], down_w.at[:, cols], down_sem.at[j])

    for j in range(tiles):
        for copy in weight_copies(j):
            copy.start()
    for j in range(pieces):
        down_copy(j).start()

    barrier = pltpu.get_barrier_semaphore()
    for mask in range(1, planes):
        pl.semaphore_signal(barrier, inc=1, device_id=lane_z(mask), device_id_type=MESH)
    pl.semaphore_signal(barrier, inc=1, device_id=lane_y, device_id_type=MESH)
    pl.semaphore_signal(barrier, inc=1, device_id=other_core, device_id_type=MESH)

    labels = lax.broadcasted_iota(jnp.int32, (own, LANES), 1)
    route = jnp.zeros((own, LANES), F32)
    for k in range(ids_ref.shape[1]):
        route += jnp.where(
            ids_ref[:, k:k + 1] == labels, gates_ref[:, k:k + 1].astype(F32), 0.0
        )
    rows_buf[0:own, width:width + LANES] = route.astype(BF16)
    block = width // scale_ref.shape[1]
    for j in range(scale_ref.shape[1]):
        cols = slice(j * block, (j + 1) * block)
        rows_buf[0:own, cols] = (
            quant_ref[:, cols].astype(F32) * scale_ref[:, j:j + 1].astype(F32)
        ).astype(BF16)

    pl.semaphore_wait(barrier, planes - 1 + 2)

    def slot(g, c, v):
        return pl.ds(g * group + (c * Y + v) * own, own)

    def gz(g):
        bit = g & -g
        return pltpu.make_async_remote_copy(
            src_ref=rows_buf.at[slot(g ^ bit, 0, 0)], dst_ref=rows_buf.at[slot(g, 0, 0)],
            send_sem=gz_send.at[g], recv_sem=gz_recv.at[g],
            device_id=lane_z(bit), device_id_type=MESH)

    last = planes - 1
    half = own // 2

    def gy(g):
        count = half if g == last else own
        return pltpu.make_async_remote_copy(
            src_ref=rows_buf.at[pl.ds(g * group, count)],
            dst_ref=rows_buf.at[pl.ds(g * group + own, count)],
            send_sem=gy_send.at[g], recv_sem=gy_recv.at[g],
            device_id=lane_y, device_id_type=MESH)

    def gz_half():
        return pltpu.make_async_remote_copy(
            src_ref=rows_buf.at[pl.ds((last ^ 1) * group + own + half, half)],
            dst_ref=rows_buf.at[pl.ds(last * group + own + half, half)],
            send_sem=gz_send.at[0], recv_sem=gz_recv.at[0],
            device_id=lane_z(1), device_id_type=MESH)

    def gc(g, v):
        return pltpu.make_async_remote_copy(
            src_ref=rows_buf.at[slot(g, 0, v)], dst_ref=rows_buf.at[slot(g, 1, v)],
            send_sem=gc_send.at[g * Y + v], recv_sem=gc_recv.at[g * Y + v],
            device_id=other_core, device_id_type=MESH)

    def children(g):
        low = g & -g if g else planes
        bit, found = 1, []
        while bit < low and g + bit < planes:
            found.append(g + bit)
            bit *= 2
        return found

    def spread(g):
        if g:
            gz(g).wait_recv()
        following = children(g) if g else []
        if g & (g - 1) == 0:
            following = ([max(2 * g, 1)] if max(2 * g, 1) < planes else []) + following
        for child in following:
            gz(child).start()
        gy(g).start()
        gc(g, 0).start()

    def pass_on(g):
        gy(g).wait_recv()
        if g == last ^ 1:
            gz_half().start()
        if g == last:
            gz_half().wait_recv()
        gc(g, 1).start()

    def sends_done(g):
        for child in children(g):
            gz(child).wait_send()
        if g == last ^ 1:
            gz_half().wait_send()
        gy(g).wait_send()
        for v in range(Y):
            gc(g, v).wait_send()

    def cols_of(p):
        return pl.ds(p * part, part)

    def rc(g, p):
        return pltpu.make_async_remote_copy(
            src_ref=rows_buf.at[pl.ds(g * group + Y * own, Y * own), cols_of(p)],
            dst_ref=from_core.at[pl.ds(g * Y * own, Y * own), cols_of(p)],
            send_sem=rc_send.at[g * pieces + p], recv_sem=rc_recv.at[g * pieces + p],
            device_id=other_core, device_id_type=MESH)

    def ry(g, p):
        return pltpu.make_async_remote_copy(
            src_ref=rows_buf.at[slot(g, 0, 1), cols_of(p)],
            dst_ref=from_y.at[pl.ds(g * own, own), cols_of(p)],
            send_sem=ry_send.at[g * pieces + p], recv_sem=ry_recv.at[g * pieces + p],
            device_id=lane_y, device_id_type=MESH)

    def rz(g, p):
        return pltpu.make_async_remote_copy(
            src_ref=rows_buf.at[slot(g, 0, 0), cols_of(p)],
            dst_ref=from_z.at[pl.ds((g - 1) * own, own), cols_of(p)],
            send_sem=rz_send.at[(g - 1) * pieces + p], recv_sem=rz_recv.at[(g - 1) * pieces + p],
            device_id=lane_z(g), device_id_type=MESH)

    def add(rows, more, more_rows, p):
        @pl.loop(0, part // TILE)
        def _(i):
            cols = pl.ds(pl.multiple_of(p * part + i * TILE, TILE), TILE)
            rows_buf[rows, cols] = (
                rows_buf[rows, cols].astype(F32) + more[more_rows, cols].astype(F32)
            ).astype(BF16)

    def core_sum(g, p):
        rc(g, p).wait_recv()
        add(slot(g, 0, 1), from_core, pl.ds((g * Y + 1) * own, own), p)
        ry(g, p).start()
        add(slot(g, 0, 0), from_core, pl.ds(g * Y * own, own), p)

    def y_sum(g, p):
        ry(g, p).wait_recv()
        add(slot(g, 0, 0), from_y, pl.ds(g * own, own), p)
        if g:
            rz(g, p).start()

    def gate_up(g):
        for v in range(Y):
            gc(g, v).wait_recv()
        rows = pl.ds(g * group, group)
        if g == 0:
            for j in range(tiles):
                for copy in weight_copies(j):
                    copy.wait()

        @pl.loop(0, tiles)
        def _(j):
            cols = pl.ds(pl.multiple_of(j * TILE, TILE), TILE)
            x = rows_buf[rows, 0:width]
            gate = jnp.dot(x, gate_w[:, cols], preferred_element_type=F32)
            up = jnp.dot(x, up_w[:, cols], preferred_element_type=F32)
            hidden[:, cols] = (gate / (1.0 + jnp.exp(-gate)) * up).astype(BF16)

    def project(g):
        sends_done(g)
        rows = pl.ds(g * group, group)
        route_all = rows_buf[rows, width:width + LANES].astype(F32)
        spots = lax.broadcasted_iota(jnp.int32, (group, LANES), 1)
        column = jnp.sum(jnp.where(spots == expert, route_all, 0.0), axis=1, keepdims=True)
        for p in range(pieces):
            if g == 0:
                down_copy(p).wait()

            @pl.loop(0, part // TILE)
            def _(i):
                cols = pl.ds(pl.multiple_of(p * part + i * TILE, TILE), TILE)
                term = jnp.dot(hidden[...], down_w[:, cols], preferred_element_type=F32)
                rows_buf[rows, cols] = (column * term).astype(BF16)

            rc(g, p).start()
            if g == last and p:
                core_sum(g, p - 1)

    spread(0)
    spread(1)
    pass_on(0)
    for g in range(planes):
        gate_up(g)
        if g + 1 < planes:
            pass_on(g + 1)
        if g + 2 < planes:
            spread(g + 2)
        if g >= 1:
            for p in range(pieces):
                core_sum(g - 1, p)
        project(g)
        if g >= 1:
            for p in range(pieces):
                y_sum(g - 1, p)
    core_sum(last, pieces - 1)
    for p in range(pieces):
        y_sum(last, p)
    for p in range(pieces):
        for g in range(1, planes):
            rz(g, p).wait_recv()

        @pl.loop(0, part // TILE)
        def _(i):
            cols = pl.ds(pl.multiple_of(p * part + i * TILE, TILE), TILE)
            total = rows_buf[0:own, cols].astype(F32)
            for g in range(1, planes):
                total += from_z[(g - 1) * own:g * own, cols].astype(F32)
            out_ref[:, cols] = total.astype(BF16)

    for g in range(planes):
        for p in range(pieces):
            rc(g, p).wait_send()
            ry(g, p).wait_send()
            if g:
                rz(g, p).wait_send()


def local(quant_rows, block_scales, expert_ids, route_gates, gate_proj, up_proj, down_proj):
    lane_total = lax.axis_size("lane")
    planes = lane_total // Y
    span_count = lane_total // EXP_GRP
    own, width = quant_rows.shape
    units = gate_proj.shape[2]
    pieces = 4
    rows = planes * Y * CORES * own
    dma = pltpu.SemaphoreType.DMA
    vmem = pl.BlockSpec(memory_space=pltpu.VMEM)
    hbm = pl.BlockSpec(memory_space=pl.ANY)
    return pl.pallas_call(
        functools.partial(kernel, planes, pieces, span_count),
        out_shape=jax.ShapeDtypeStruct((own, width), BF16),
        in_specs=[vmem] * 4 + [hbm] * 3,
        out_specs=vmem,
        scratch_shapes=[
            pltpu.VMEM((width, units), BF16),
            pltpu.VMEM((width, units), BF16),
            pltpu.VMEM((units, width), BF16),
            pltpu.VMEM((rows, width + LANES), BF16),
            pltpu.VMEM((Y * CORES * own, units), BF16),
            pltpu.VMEM((planes * Y * own, width), BF16),
            pltpu.VMEM((planes * own, width), BF16),
            pltpu.VMEM(((planes - 1) * own, width), BF16),
            dma((units // TILE,)), dma((units // TILE,)), dma((pieces,)),
            dma((planes,)), dma((planes,)),
            dma((planes,)), dma((planes,)),
            dma((planes * Y,)), dma((planes * Y,)),
            dma((planes * pieces,)), dma((planes * pieces,)),
            dma((planes * pieces,)), dma((planes * pieces,)),
            dma((planes * pieces,)), dma((planes * pieces,)),
        ],
        compiler_params=pltpu.CompilerParams(
            collective_id=0, has_side_effects=True, vmem_limit_bytes=62 << 20
        ),
    )(quant_rows, block_scales, expert_ids, route_gates, gate_proj, up_proj, down_proj)


def solution(mesh):
    rows = P(("parts", "node", "lane"), None)
    weights = P(("node", "lane"), None, None)
    return jax.shard_map(
        local,
        mesh=mesh,
        in_specs=(rows,) * 4 + (weights,) * 3,
        out_specs=rows,
        check_vma=False,
    )
```

```python
import functools

import jax
import jax.numpy as jnp
from jax import lax
from jax.experimental import pallas as pl
from jax.experimental.pallas import tpu as pltpu
from jax.sharding import PartitionSpec as P

EXP_GRP = 4
Y = 2
CORES = 2
LANES = 128
TILE = 256
MESH = pl.DeviceIdType.MESH
F32 = jnp.float32
BF16 = jnp.bfloat16


def flip(value, bit):
    return value + bit - 2 * bit * ((value // bit) % 2)


def flip_all(value, mask):
    bit = 1
    while bit <= mask:
        if mask & bit:
            value = flip(value, bit)
        bit *= 2
    return value


def kernel(
    planes, pieces, span_count,
    quant_ref, scale_ref, ids_ref, gates_ref, gate_hbm, up_hbm, down_hbm,
    out_ref,
    gate_w, up_w, down_w, rows_buf, hidden, from_core, from_y, from_z,
    gate_sem, up_sem, down_sem,
    gz_send, gz_recv, gy_send, gy_recv, gc_send, gc_recv,
    rc_send, rc_recv, ry_send, ry_recv, rz_send, rz_recv,
):
    own, width = quant_ref.shape
    units = gate_w.shape[1]
    tiles = units // TILE
    group = CORES * Y * own
    part = width // pieces
    node, lane = lax.axis_index("node"), lax.axis_index("lane")
    z, y = lane // Y, lane % Y
    expert = node * EXP_GRP + lane // span_count

    def lane_z(mask):
        return {"lane": flip_all(z, mask) * Y + y}

    lane_y = {"lane": z * Y + (1 - y)}
    other_core = {"node": 1 - node}

    order = list(range(1, planes)) + [0]

    def weight_copies(j):
        cols = pl.ds(j * TILE, TILE)
        return (
            pltpu.make_async_copy(gate_hbm.at[0, :, cols], gate_w.at[:, cols], gate_sem.at[j]),
            pltpu.make_async_copy(up_hbm.at[0, :, cols], up_w.at[:, cols], up_sem.at[j]),
        )

    def down_copy(j):
        cols = pl.ds(j * part, part)
        return pltpu.make_async_copy(down_hbm.at[0, :, cols], down_w.at[:, cols], down_sem.at[j])

    for j in range(tiles):
        for copy in weight_copies(j):
            copy.start()
    for j in range(pieces):
        down_copy(j).start()

    barrier = pltpu.get_barrier_semaphore()
    for mask in range(1, planes):
        pl.semaphore_signal(barrier, inc=1, device_id=lane_z(mask), device_id_type=MESH)
    pl.semaphore_signal(barrier, inc=1, device_id=lane_y, device_id_type=MESH)
    pl.semaphore_signal(barrier, inc=1, device_id=other_core, device_id_type=MESH)

    labels = lax.broadcasted_iota(jnp.int32, (own, LANES), 1)
    route = jnp.zeros((own, LANES), F32)
    for k in range(ids_ref.shape[1]):
        route += jnp.where(
            ids_ref[:, k:k + 1] == labels, gates_ref[:, k:k + 1].astype(F32), 0.0
        )
    rows_buf[0:own, width:width + LANES] = route.astype(BF16)
    block = width // scale_ref.shape[1]
    for j in range(scale_ref.shape[1]):
        cols = slice(j * block, (j + 1) * block)
        rows_buf[0:own, cols] = (
            quant_ref[:, cols].astype(F32) * scale_ref[:, j:j + 1].astype(F32)
        ).astype(BF16)

    pl.semaphore_wait(barrier, planes - 1 + 2)

    def slot(g, c, v):
        return pl.ds(g * group + (c * Y + v) * own, own)

    def gz(g):
        bit = g & -g
        return pltpu.make_async_remote_copy(
            src_ref=rows_buf.at[slot(g ^ bit, 0, 0)], dst_ref=rows_buf.at[slot(g, 0, 0)],
            send_sem=gz_send.at[g], recv_sem=gz_recv.at[g],
            device_id=lane_z(bit), device_id_type=MESH)

    def gy(g):
        return pltpu.make_async_remote_copy(
            src_ref=rows_buf.at[slot(g, 0, 0)], dst_ref=rows_buf.at[slot(g, 0, 1)],
            send_sem=gy_send.at[g], recv_sem=gy_recv.at[g],
            device_id=lane_y, device_id_type=MESH)

    def gc(g, v):
        return pltpu.make_async_remote_copy(
            src_ref=rows_buf.at[slot(g, 0, v)], dst_ref=rows_buf.at[slot(g, 1, v)],
            send_sem=gc_send.at[g * Y + v], recv_sem=gc_recv.at[g * Y + v],
            device_id=other_core, device_id_type=MESH)

    def children(g):
        low = g & -g if g else planes
        bit, found = 1, []
        while bit < low and g + bit < planes:
            found.append(g + bit)
            bit *= 2
        return found

    def spread(g):
        if g:
            gz(g).wait_recv()
        for child in children(g):
            gz(child).start()
        gy(g).start()
        gc(g, 0).start()

    def pass_on(g):
        gy(g).wait_recv()
        gc(g, 1).start()

    def sends_done(g):
        for child in children(g):
            gz(child).wait_send()
        gy(g).wait_send()
        for v in range(Y):
            gc(g, v).wait_send()

    def cols_of(p):
        return pl.ds(p * part, part)

    def rc(g, p):
        return pltpu.make_async_remote_copy(
            src_ref=rows_buf.at[pl.ds(g * group + Y * own, Y * own), cols_of(p)],
            dst_ref=from_core.at[pl.ds(g * Y * own, Y * own), cols_of(p)],
            send_sem=rc_send.at[g * pieces + p], recv_sem=rc_recv.at[g * pieces + p],
            device_id=other_core, device_id_type=MESH)

    def ry(g, p):
        return pltpu.make_async_remote_copy(
            src_ref=rows_buf.at[slot(g, 0, 1), cols_of(p)],
            dst_ref=from_y.at[pl.ds(g * own, own), cols_of(p)],
            send_sem=ry_send.at[g * pieces + p], recv_sem=ry_recv.at[g * pieces + p],
            device_id=lane_y, device_id_type=MESH)

    def rz(g, p):
        return pltpu.make_async_remote_copy(
            src_ref=rows_buf.at[slot(g, 0, 0), cols_of(p)],
            dst_ref=from_z.at[pl.ds((g - 1) * own, own), cols_of(p)],
            send_sem=rz_send.at[(g - 1) * pieces + p], recv_sem=rz_recv.at[(g - 1) * pieces + p],
            device_id=lane_z(g), device_id_type=MESH)

    def add(rows, more, more_rows, p):
        @pl.loop(0, part // TILE)
        def _(i):
            cols = pl.ds(pl.multiple_of(p * part + i * TILE, TILE), TILE)
            rows_buf[rows, cols] = (
                rows_buf[rows, cols].astype(F32) + more[more_rows, cols].astype(F32)
            ).astype(BF16)

    def core_sum(g, p):
        rc(g, p).wait_recv()
        add(slot(g, 0, 1), from_core, pl.ds((g * Y + 1) * own, own), p)
        ry(g, p).start()
        add(slot(g, 0, 0), from_core, pl.ds(g * Y * own, own), p)

    def y_sum(g, p):
        ry(g, p).wait_recv()
        add(slot(g, 0, 0), from_y, pl.ds(g * own, own), p)
        if g:
            rz(g, p).start()

    def gate_up(g):
        for v in range(Y):
            gc(g, v).wait_recv()
        rows = pl.ds(g * group, group)
        if g == order[0]:
            for j in range(tiles):
                for copy in weight_copies(j):
                    copy.wait()

        @pl.loop(0, tiles)
        def _(j):
            cols = pl.ds(pl.multiple_of(j * TILE, TILE), TILE)
            x = rows_buf[rows, 0:width]
            gate = jnp.dot(x, gate_w[:, cols], preferred_element_type=F32)
            up = jnp.dot(x, up_w[:, cols], preferred_element_type=F32)
            hidden[:, cols] = (gate / (1.0 + jnp.exp(-gate)) * up).astype(BF16)

    def project(g):
        sends_done(g)
        rows = pl.ds(g * group, group)
        route_all = rows_buf[rows, width:width + LANES].astype(F32)
        spots = lax.broadcasted_iota(jnp.int32, (group, LANES), 1)
        column = jnp.sum(jnp.where(spots == expert, route_all, 0.0), axis=1, keepdims=True)
        for p in range(pieces):
            if g == order[0]:
                down_copy(p).wait()

            @pl.loop(0, part // TILE)
            def _(i):
                cols = pl.ds(pl.multiple_of(p * part + i * TILE, TILE), TILE)
                term = jnp.dot(hidden[...], down_w[:, cols], preferred_element_type=F32)
                rows_buf[rows, cols] = (column * term).astype(BF16)

            rc(g, p).start()

    for g in range(min(planes, 3)):
        spread(g)
    for g in range(2):
        pass_on(g)
    for i, g in enumerate(order):
        gate_up(g)
        if 3 + i < planes:
            spread(3 + i)
        if 2 + i < planes:
            pass_on(2 + i)
        for back, step in ((1, core_sum), (2, y_sum)):
            if i >= back:
                for p in range(pieces):
                    step(order[i - back], p)
        project(g)
    for step, g in ((core_sum, order[-1]), (y_sum, order[-2]), (y_sum, order[-1])):
        for p in range(pieces):
            step(g, p)
    for p in range(pieces):
        for g in range(1, planes):
            rz(g, p).wait_recv()

        @pl.loop(0, part // TILE)
        def _(i):
            cols = pl.ds(pl.multiple_of(p * part + i * TILE, TILE), TILE)
            total = rows_buf[0:own, cols].astype(F32)
            for g in range(1, planes):
                total += from_z[(g - 1) * own:g * own, cols].astype(F32)
            out_ref[:, cols] = total.astype(BF16)

    for g in range(planes):
        for p in range(pieces):
            rc(g, p).wait_send()
            ry(g, p).wait_send()
            if g:
                rz(g, p).wait_send()


def local(quant_rows, block_scales, expert_ids, route_gates, gate_proj, up_proj, down_proj):
    lane_total = lax.axis_size("lane")
    planes = lane_total // Y
    span_count = lane_total // EXP_GRP
    own, width = quant_rows.shape
    units = gate_proj.shape[2]
    pieces = 4
    rows = planes * Y * CORES * own
    dma = pltpu.SemaphoreType.DMA
    vmem = pl.BlockSpec(memory_space=pltpu.VMEM)
    hbm = pl.BlockSpec(memory_space=pl.ANY)
    return pl.pallas_call(
        functools.partial(kernel, planes, pieces, span_count),
        out_shape=jax.ShapeDtypeStruct((own, width), BF16),
        in_specs=[vmem] * 4 + [hbm] * 3,
        out_specs=vmem,
        scratch_shapes=[
            pltpu.VMEM((width, units), BF16),
            pltpu.VMEM((width, units), BF16),
            pltpu.VMEM((units, width), BF16),
            pltpu.VMEM((rows, width + LANES), BF16),
            pltpu.VMEM((Y * CORES * own, units), BF16),
            pltpu.VMEM((planes * Y * own, width), BF16),
            pltpu.VMEM((planes * own, width), BF16),
            pltpu.VMEM(((planes - 1) * own, width), BF16),
            dma((units // TILE,)), dma((units // TILE,)), dma((pieces,)),
            dma((planes,)), dma((planes,)),
            dma((planes,)), dma((planes,)),
            dma((planes * Y,)), dma((planes * Y,)),
            dma((planes * pieces,)), dma((planes * pieces,)),
            dma((planes * pieces,)), dma((planes * pieces,)),
            dma((planes * pieces,)), dma((planes * pieces,)),
        ],
        compiler_params=pltpu.CompilerParams(
            collective_id=0, has_side_effects=True, vmem_limit_bytes=62 << 20
        ),
    )(quant_rows, block_scales, expert_ids, route_gates, gate_proj, up_proj, down_proj)


def solution(mesh):
    rows = P(("parts", "node", "lane"), None)
    weights = P(("node", "lane"), None, None)
    return jax.shard_map(
        local,
        mesh=mesh,
        in_specs=(rows,) * 4 + (weights,) * 3,
        out_specs=rows,
        check_vma=False,
    )
```
